128 devices in a mesh: section: 2 (over core), ctx: 64 (over z, x, y).
Axes of the slice: x: 4, y: 4, z: 4, core: 2. Of those that a mesh axis runs over, the one named last changes fastest.
Arguments:
- queries: bfloat16 [2, 32768, 2048], P('section', 'ctx'), may hold values from -20 to 20
- nb_kv: bfloat16 [2, 512, 2, 128, 1024], P('section', 'ctx'), may hold values from -6 to 6
- out_grad: bfloat16 [32768, 2048], P('ctx'), may hold values from -6 to 6
- kv_weight: bfloat16 [2, 896, 1024], P('section'), may hold values from -0.1875 to 0.1875
- nb_owner: int32 [512, 2], P('ctx'), may hold values from 0 to 63, all different within a row; in each aligned block of 8 rows (0 to 7, 8 to 15, ...) at most 2 rows name the same one
- nb_row: int32 [512, 2], P('ctx'), may hold values from 0 to 15
Outputs:
- input_grads: bfloat16 [2, 32768, 2048], P('section', 'ctx')
- enc_grad: bfloat16 [1024, 128, 896], P('ctx', None, 'section')
The draws below stay inside these ranges and needn't reach their ends.
Inputs may be any that keep to these rules, and one draw needn't show every extreme that they name: `nb_owner`: the 2 neighbours of a span have different owners. Among the spans of one device (aligned blocks of 8 spans) no owner is named more than 2 times, a bound that some block reaches.
All inputs are finite; a program needn't handle non-finite values.
Results may differ from the reference program's by a relative error of at most 0.0076.
Values may be sent and summed in bfloat16 or wider, within the bound.
A program may use at most 192 MiB of HBM per device.

```python
import math
import jax
import jax.numpy as jnp
import numpy as np
from jax import lax

HEADS = 16
KV_HEADS = 4
HDIM = 128
D_ENC = 896
SPAN = 64
NB = 2
NBLEN = 128
CAP = 2
CH_DEV = 8
SECTIONS = 2
SPANS = 512
TOKENS = 32768
ENC_DEV = 16
ENC = 1024
INNER = 2048
KVW = 512
N_SECTION = 2
N_CTX = 64


def draw_queries(key, part):
    full_shape = (SECTIONS, SPANS, SPAN, INNER)
    samples = jnp.clip(1.5 * jax.random.normal(jax.random.fold_in(key, 1), full_shape, jnp.float32), -9.0, 9.0)
    return samples.reshape(SECTIONS, TOKENS, INNER).astype(jnp.bfloat16)


def draw_nb_kv(key, part):
    full_shape = (SECTIONS, SPANS, NB, NBLEN, 2 * KVW)
    samples = jnp.clip(jax.random.normal(jax.random.fold_in(key, 2), full_shape, jnp.float32), -6.0, 6.0)
    return samples.astype(jnp.bfloat16)


def set_ends(result, key, least, high):
    longest = result.shape.index(max(result.shape))
    spots = []
    for shift in (0, 1):
        where = [jax.random.randint(jax.random.fold_in(key, axis), (), 0, length) for axis, length in enumerate(result.shape)]
        where[longest] = (where[longest] + shift) % result.shape[longest]
        spots.append(tuple(where))
    return result.at[spots[0]].set(least).at[spots[1]].set(high)


def block_levels(stream_key, extent, split, low, largest):
    def one(dim, parts):
        draws = jax.random.uniform(jax.random.fold_in(jax.random.fold_in(stream_key, 6), dim), (parts,), jnp.float32, low / len(split), largest / len(split))
        return jnp.repeat(jnp.exp(draws), extent[dim] // parts).reshape((-1,) + (1,) * (len(extent) - dim - 1))

    gain = one(*split[0])
    for cut in split[1:]:
        gain = gain * one(*cut)
    return gain


def rank_bounds(number_of, lean):
    portions = [(1 << 20) // math.isqrt(standing ** lean) + 1 for standing in range(1, number_of + 1)]
    scale = 1 + sum(portions) // (1 << 30)
    return np.cumsum(np.array([max(1, weight // scale) for weight in portions]))


def skewed_ids(key, shape, amount, lean):
    listing = rank_bounds(amount, lean)
    ticket = jax.random.randint(jax.random.fold_in(key, 1), shape, 0, int(listing[amount - 1]))
    standing = jnp.searchsorted(jnp.asarray(listing, jnp.int32), ticket, side="right")
    return jax.random.permutation(jax.random.fold_in(key, 2), amount)[standing].astype(jnp.int32)


def assign_block(rng, own, number, rows, count, top, bound, slope):
    ranking = jax.random.permutation(rng, count)
    crowded, usual = load_shares(count, rows * top, bound, slope, True), load_shares(count, rows * top, bound, slope, False)
    places = jnp.arange(count)

    def named(lengths, offset_by):
        used = int((lengths > 0).sum())
        fixed = max(1, used // 4)
        passed = fixed + (places - fixed + offset_by * (used - fixed)) % max(1, count - fixed)
        return jnp.zeros((count,), jnp.int32).at[ranking[jnp.where(places < fixed, places, passed)]].set(jnp.asarray(lengths, jnp.int32))

    lengths = jnp.where(number % 4 == 0, named(crowded, number // 4), named(usual, number - number // 4 - 1))
    mixed = jax.random.permutation(jax.random.fold_in(own, 3), count)
    giver, taker = mixed[0:count // 2 * 2:2], mixed[1:count // 2 * 2:2]
    slack = jnp.minimum(lengths[giver] - 1, bound - lengths[taker]) // 2
    slack = jnp.where((giver == ranking[0]) | (taker == ranking[0]) | (lengths[taker] == 0), 0, jnp.maximum(slack, 0))
    passed = jax.random.randint(jax.random.fold_in(own, 4), (count // 2,), 0, 1 << 20) % (slack + 1)
    lengths = lengths.at[giver].add(-passed).at[taker].add(passed)
    members = jnp.searchsorted(jnp.cumsum(lengths), jnp.arange(rows * top), side="right").astype(jnp.int32)
    table = members.reshape(top, rows).T
    table = table[jax.random.permutation(jax.random.fold_in(own, 1), rows)]
    offset_by = jax.random.randint(jax.random.fold_in(own, 2), (rows, 1), 0, top)
    return jnp.take_along_axis(table, (jnp.arange(top)[None, :] + offset_by) % top, axis=1)


def load_shares(count, total, most, slope, full):
    weights = [(1 << 20) // math.isqrt(rank ** slope) + 1 for rank in range(1, count + 1)]
    largest = most if full else min(most, max(-(-total // count), total * weights[0] // sum(weights)))
    least = 1 if total - largest >= count - 1 else 0
    given, spare = [largest] + [least] * (count - 1), total - largest - least * (count - 1)
    while spare > 0:
        candidates = [i for i in range(1, count) if given[i] < largest] or [i for i in range(1, count) if given[i] < most]
        whole, left = sum([weights[i] for i in candidates]), spare
        for i in candidates:
            addition = min(most - given[i], max(1, left * weights[i] // whole), spare)
            given[i] = given[i] + addition
            spare = spare - addition
    return np.array(given)


def normal_values(own_key, shape, spread, most, split=(), held_as=jnp.bfloat16):
    loudness = block_levels(own_key, shape, split, -0.22, 0.18) if split else 1.0
    result = jax.random.normal(own_key, shape, jnp.float32) * spread * loudness
    return jnp.minimum(jnp.maximum(result, -most), most).astype(held_as)


def setup_inputs(seed: int = 0) -> dict:
    streams_of = jax.random.split(jax.random.key(seed), 7)
    queries = draw_queries(jax.random.fold_in(streams_of[6], 71), 0)
    nb_kv = draw_nb_kv(jax.random.fold_in(streams_of[6], 71), 0)
    out_grad = normal_values(streams_of[2], (TOKENS, INNER), 1.0, 6.0, ((0, 64),))
    kv_weight = normal_values(streams_of[3], (SECTIONS, D_ENC, 2 * KVW), (2 * KVW) ** -0.5, 0.1875, ((0, 2),))
    nb_owner_keys = jax.random.split(jax.random.fold_in(streams_of[4], 1), SPANS // CH_DEV)
    nb_owner_turns = jax.random.permutation(jax.random.fold_in(streams_of[4], 3), SPANS // CH_DEV)
    nb_owner = jax.vmap(lambda own, number: assign_block(jax.random.fold_in(streams_of[4], 2), own, number, CH_DEV, N_CTX, NB, CAP, 2))(nb_owner_keys, nb_owner_turns).reshape((SPANS, NB))
    nb_row = set_ends(skewed_ids(streams_of[5], (SPANS, NB), ENC_DEV, 2), jax.random.fold_in(streams_of[5], 3), 0, ENC_DEV - 1).astype(jnp.int32)
    return {"queries": queries, "nb_kv": nb_kv, "out_grad": out_grad, "kv_weight": kv_weight, "nb_owner": nb_owner, "nb_row": nb_row}


def span_backward(query_rows, cotangent, neighbour_kv):
    group_size = HEADS // KV_HEADS
    kv_width = KV_HEADS * HDIM
    score_scale = 1.0 / math.sqrt(HDIM)
    query_heads = query_rows.astype(jnp.float32).reshape(SPAN, KV_HEADS, group_size, HDIM)
    grad_heads = cotangent.astype(jnp.float32).reshape(SPAN, KV_HEADS, group_size, HDIM)
    key_rows = neighbour_kv[..., :kv_width].astype(jnp.float32).reshape(NB * NBLEN, KV_HEADS, HDIM)
    value_rows = neighbour_kv[..., kv_width:].astype(jnp.float32).reshape(NB * NBLEN, KV_HEADS, HDIM)
    scores = jnp.einsum('qhgd,khd->hgqk', query_heads, key_rows) * score_scale
    row_peak = lax.optimization_barrier(jnp.max(scores, axis=-1, keepdims=True))
    weights_raw = jnp.exp(scores - row_peak)
    probabilities = weights_raw / lax.optimization_barrier(jnp.sum(weights_raw, axis=-1, keepdims=True))
    probs_low = lax.optimization_barrier(probabilities.astype(jnp.bfloat16)).astype(jnp.float32)
    outputs = jnp.einsum('hgqk,khd->qhgd', probs_low, value_rows)
    row_dot = lax.optimization_barrier(jnp.sum(grad_heads * outputs, axis=-1))
    value_grad = jnp.einsum('hgqk,qhgd->khd', probs_low, grad_heads)
    prob_grad = jnp.einsum('qhgd,khd->hgqk', grad_heads, value_rows)
    score_grad = probabilities * (prob_grad - jnp.transpose(row_dot, (1, 2, 0))[..., None])
    score_low = lax.optimization_barrier(score_grad.astype(jnp.bfloat16)).astype(jnp.float32)
    query_grad = jnp.einsum('hgqk,khd->qhgd', score_low, key_rows) * score_scale
    key_grad = jnp.einsum('hgqk,qhgd->khd', score_low, query_heads) * score_scale
    input_grad = (grad_heads.reshape(SPAN, -1) + query_grad.reshape(SPAN, -1)).astype(jnp.bfloat16)
    kv_grad = jnp.concatenate([key_grad.reshape(NB, NBLEN, kv_width), value_grad.reshape(NB, NBLEN, kv_width)], axis=-1).astype(jnp.bfloat16)
    return (input_grad, kv_grad)

def block_backward(packed):
    return jax.vmap(span_backward)(packed[0], packed[1], packed[2])

def reference(queries, nb_kv, out_grad, kv_weight, nb_owner, nb_row):
    encoder_rows = (nb_owner * ENC_DEV + nb_row).reshape(-1).astype(jnp.int32)
    block_size = math.gcd(SPANS, 16)
    block_total = SPANS // block_size
    cotangent = out_grad
    collected = []
    enc_total = jnp.zeros((ENC, NBLEN, D_ENC), jnp.float32)
    for layer_index in range(N_SECTION - 1, -1, -1):
        layer_queries = queries[layer_index].reshape(block_total, block_size, SPAN, INNER)
        layer_grads = cotangent.reshape(block_total, block_size, SPAN, INNER)
        layer_kv = nb_kv[layer_index].reshape(block_total, block_size, NB, NBLEN, 2 * KVW)
        input_grad, kv_grad = lax.map(block_backward, (layer_queries, layer_grads, layer_kv))
        row_sum = jnp.zeros((ENC, NBLEN, 2 * KVW), jnp.float32).at[encoder_rows].add(kv_grad.reshape(SPANS * NB, NBLEN, 2 * KVW).astype(jnp.float32))
        layer_enc = jnp.einsum('rtc,ec->rte', row_sum, kv_weight[layer_index].astype(jnp.float32), precision=lax.Precision.HIGHEST).astype(jnp.bfloat16)
        enc_total = enc_total + layer_enc.astype(jnp.float32)
        cotangent = input_grad.reshape(TOKENS, INNER)
        collected = [cotangent] + collected
    return (jnp.stack(collected), enc_total.astype(jnp.bfloat16))
```

```python
import functools
import math

import jax
import jax.numpy as jnp
from jax import lax
from jax.experimental import pallas as pl
from jax.experimental.pallas import tpu as pltpu
from jax.sharding import PartitionSpec as P

HEADS = 16
KV_HEADS = 4
GROUP = HEADS // KV_HEADS
HDIM = 128
SPAN = 64
NB = 2
NBLEN = 128
CAP = 2
RING = 4
ROWS_DEV = 16
STRIDES = (16, 4, 1)
HALF = 448
PARTS = ((0, 160), (160, 144), (304, 144))
LAG_SUM = 2
LAG_FWD = 4
F32 = jnp.float32
BF16 = jnp.bfloat16
MESH = pl.DeviceIdType.MESH


def axis_step(axis, delta):
    me = lax.axis_index("ctx")
    stride = STRIDES[axis]
    coord = lax.rem(me // stride, RING)
    return me + (lax.rem(coord + delta + RING, RING) - coord) * stride


def greet(devices):
    barrier = pltpu.get_barrier_semaphore()
    for device in devices:
        pl.semaphore_signal(barrier, inc=1, device_id=device, device_id_type=MESH)
    pl.semaphore_wait(barrier, len(devices))


def neighbours():
    sec = lax.axis_index("section")
    return [[(sec, axis_step(a, 1)), (sec, axis_step(a, -1))] for a in range(3)]


def nt(a, b):
    return lax.dot_general(a, b, (((1,), (1,)), ((), ())), preferred_element_type=F32)


def nn(a, b):
    return lax.dot_general(a, b, (((1,), (0,)), ((), ())), preferred_element_type=F32)


def tn(a, b):
    return lax.dot_general(a, b, (((0,), (0,)), ((), ())), preferred_element_type=F32)


def pack_half(prod, n):
    base = n * NBLEN
    blocks = [prod[base : base + NBLEN, j * 128 : (j + 1) * 128] for j in range(3)]
    lane = lax.broadcasted_iota(jnp.int32, (NBLEN // 2, 128), 1)
    tail = jnp.where(
        lane < 64,
        prod[base : base + NBLEN // 2, 384:512],
        prod[base + NBLEN // 2 : base + NBLEN, 384:512],
    )
    return jnp.concatenate(blocks + [tail], axis=0)


def relay_kernel(
    q_hbm, kv_hbm, og_hbm, w_hbm, ig_hbm, gath_hbm,
    q_v, kv_v, cot_v, ig_v, w_v, kvg_v, own_v, xsend_v, xrecv_v, gown_v,
    ld_sem, w_sem, out_sem, cs_send, cs_recv, xs_send, xs_recv, gl_sem,
    ag_send, ag_recv, fw_send, fw_recv,
):
    spans = kv_v.shape[0]
    sec = lax.axis_index("section")
    me = lax.axis_index("ctx")
    partner = (1 - sec, me)
    near = neighbours()
    scale = 1.0 / math.sqrt(HDIM)

    def load(c, which):
        hbm, vmem = ((q_hbm, q_v), (kv_hbm, kv_v), (og_hbm, cot_v))[which]
        return pltpu.make_async_copy(hbm.at[c], vmem.at[c], ld_sem.at[c, which])

    def load_w(half, piece):
        if piece == 0:
            source, target = pl.ds(half * HALF, HALF), pl.ds(0, HALF)
        else:
            source, target = pl.ds(half * HALF + 384, 64), pl.ds(HALF, 64)
        return pltpu.make_async_copy(w_hbm.at[source], w_v.at[half, target], w_sem.at[half, piece])

    def out_copy(c):
        return pltpu.make_async_copy(ig_v.at[c], ig_hbm.at[c], out_sem.at[c])

    def cot_copy(c):
        return pltpu.make_async_remote_copy(
            ig_v.at[c], cot_v.at[c], cs_send.at[c], cs_recv.at[c], device_id=partner, device_id_type=MESH
        )

    def proj_copy(c):
        return pltpu.make_async_remote_copy(
            xsend_v.at[c], xrecv_v.at[c], xs_send.at[c], xs_recv.at[c], device_id=partner, device_id_type=MESH
        )

    def own_copy(c):
        return pltpu.make_async_copy(gown_v.at[c], gath_hbm.at[0, c], gl_sem.at[c])

    def gather_copy(c, p, way):
        rows = pl.ds(*PARTS[p])
        return pltpu.make_async_remote_copy(
            gown_v.at[c, :, rows], gath_hbm.at[1 + 2 * way, c, :, rows],
            ag_send.at[c, p, way], ag_recv.at[c, p, way], device_id=near[p][way], device_id_type=MESH,
        )

    def forward_copy(c, p, way):
        rows = pl.ds(*PARTS[p])
        return pltpu.make_async_remote_copy(
            gath_hbm.at[1 + 2 * way, c, way, rows], gath_hbm.at[2, c, way, rows],
            fw_send.at[c, p, way], fw_recv.at[c, p, way], device_id=near[p][way], device_id_type=MESH,
        )

    def start_loads(c, carry):
        load(c, 0).start()
        load(c, 1).start()

        @pl.when(sec == 1)
        def _():
            load(c, 2).start()

        return carry

    lax.fori_loop(0, 1, start_loads, 0)
    for half in range(2):
        for piece in range(2):
            load_w(half, piece).start()
    lax.fori_loop(1, spans, start_loads, 0)

    greet([partner] + [d for pair in near for d in pair])

    for half in range(2):
        for piece in range(2):
            load_w(half, piece).wait()

    def attend(c):
        for h in range(KV_HEADS):
            heads = [slice((h * GROUP + g) * HDIM, (h * GROUP + g + 1) * HDIM) for g in range(GROUP)]
            cols = slice(h * HDIM, (h + 1) * HDIM)
            vcols = slice((KV_HEADS + h) * HDIM, (KV_HEADS + h + 1) * HDIM)
            q = jnp.concatenate([q_v[c, :, s] for s in heads], axis=0)
            g = jnp.concatenate([cot_v[c, :, s] for s in heads], axis=0)
            k = kv_v[c, :, cols]
            v = kv_v[c, :, vcols]
            s = nt(k, q) * (scale * math.log2(math.e))
            e = jnp.exp2(s - jnp.max(s, axis=0, keepdims=True))
            prob = e * (1.0 / jnp.sum(e, axis=0, keepdims=True))
            low = prob.astype(BF16)
            dp = nt(v, g)
            dot = jnp.sum(low.astype(F32) * dp, axis=0, keepdims=True)
            ds = (prob * (dp - dot)).astype(BF16)
            kvg_v[:, vcols] = nn(low, g).astype(BF16)
            kvg_v[:, cols] = (nn(ds, q) * scale).astype(BF16)
            grad = (g.astype(F32) + tn(ds, k) * scale).astype(BF16)
            for i, col in enumerate(heads):
                ig_v[c, :, col] = grad[i * SPAN : (i + 1) * SPAN]

    def project(c):
        kvg = kvg_v[...]
        other = nt(kvg, w_v[1 - sec])
        for n in range(NB):
            xsend_v[c, n] = pack_half(other, n).astype(BF16)
        proj_copy(c).start()
        mine = nt(kvg, w_v[sec])
        for n in range(NB):
            own_v[c, n] = pack_half(mine, n)

    def step(t, carry):
        c = t - (1 - sec)
        live = (c >= 0) & (c < spans)

        @pl.when(live)
        def _():
            load(c, 0).wait()
            load(c, 1).wait()

            @pl.when(sec == 1)
            def _():
                load(c, 2).wait()

            @pl.when(sec == 0)
            def _():
                cot_copy(c).wait_recv()

            attend(c)
            out_copy(c).start()

            @pl.when(sec == 1)
            def _():
                cot_copy(c).start()

        s = t - LAG_SUM

        @pl.when((s >= 0) & (s < spans))
        def _():
            proj_copy(s).wait_recv()
            for n in range(NB):
                gown_v[s, n] = (own_v[s, n] + xrecv_v[s, n].astype(F32)).astype(BF16)
            for p in range(3):
                for way in range(2):
                    gather_copy(s, p, way).start()
            own_copy(s).start()

        f = t - LAG_FWD

        @pl.when((f >= 0) & (f < spans))
        def _():
            for p in range(3):
                for way in range(2):
                    gather_copy(f, p, way).wait_recv()
                    forward_copy(f, p, way).start()

        @pl.when(live)
        def _():
            project(c)

        return carry

    lax.fori_loop(0, spans + LAG_FWD, step, 0)

    def finish(c, carry):
        out_copy(c).wait()

        @pl.when(sec == 1)
        def _():
            cot_copy(c).wait_send()

        proj_copy(c).wait_send()
        own_copy(c).wait()
        for p in range(3):
            for way in range(2):
                gather_copy(c, p, way).wait_send()
                forward_copy(c, p, way).wait()
        return carry

    lax.fori_loop(0, spans, finish, 0)


def relay(queries, nb_kv, out_grad, weight):
    spans = nb_kv.shape[0]
    kvw2 = nb_kv.shape[-1]
    inner = queries.shape[-1]
    dma = pltpu.SemaphoreType.DMA
    item = (spans, NB, HALF, 128)
    any_spec = pl.BlockSpec(memory_space=pl.ANY)
    return pl.pallas_call(
        relay_kernel,
        name="relay",
        out_shape=(
            jax.ShapeDtypeStruct((spans, SPAN, inner), BF16),
            jax.ShapeDtypeStruct((RING,) + item, BF16),
        ),
        in_specs=[any_spec] * 4,
        out_specs=(any_spec, any_spec),
        scratch_shapes=[
            pltpu.VMEM((spans, SPAN, inner), BF16),
            pltpu.VMEM((spans, NB * NBLEN, kvw2), BF16),
            pltpu.VMEM((spans, SPAN, inner), BF16),
            pltpu.VMEM((spans, SPAN, inner), BF16),
            pltpu.VMEM((2, 512, kvw2), BF16),
            pltpu.VMEM((NB * NBLEN, kvw2), BF16),
            pltpu.VMEM(item, F32),
            pltpu.VMEM(item, BF16),
            pltpu.VMEM(item, BF16),
            pltpu.VMEM(item, BF16),
            dma((spans, 3)),
            dma((2, 2)),
            dma((spans,)),
            dma((spans,)),
            dma((spans,)),
            dma((spans,)),
            dma((spans,)),
            dma((spans,)),
            dma((spans, 3, 2)),
            dma((spans, 3, 2)),
            dma((spans, 3, 2)),
            dma((spans, 3, 2)),
        ],
        compiler_params=pltpu.CompilerParams(
            collective_id=0, has_side_effects=True, vmem_limit_bytes=48 * 2**20
        ),
        cost_estimate=pl.CostEstimate(flops=7 * 10**9, bytes_accessed=20 * 10**6, transcendentals=2**21),
    )(
        queries.reshape(spans, SPAN, inner),
        nb_kv.reshape(spans, NB * NBLEN, kvw2),
        out_grad.reshape(spans, SPAN, inner),
        weight,
    )


def route_kernel(cap, table, gath_hbm, out_ref, prefix, *refs):
    names = ("gath", "msend", "mrecv", "mtrans", "psend", "rtrans", "rrecv")
    buf = {name: refs[3 * i : 3 * i + 3] for i, name in enumerate(names)}
    (ld_sem, m_send, m_recv, mt_send, mt_recv, mf_send, mf_recv,
     rt_send, rt_recv, r0_send, r0_recv, r1_send, r1_recv) = refs[3 * len(names) :]
    total = RING * cap
    half = cap // 2
    near = neighbours()
    first, order, keep, last = 0, 3 * total, 6 * total, 9 * total

    def load(p):
        return pltpu.make_async_copy(gath_hbm.at[:, pl.ds(*PARTS[p])], buf["gath"][p], ld_sem.at[p])

    def remote(p, way, src, dst, send, recv):
        return pltpu.make_async_remote_copy(
            src, dst, send.at[p, way], recv.at[p, way], device_id=near[(p + 1) % 3][way], device_id_type=MESH
        )

    def remote3(p, way, src, dst, send, recv):
        return pltpu.make_async_remote_copy(
            src, dst, send.at[p, way], recv.at[p, way], device_id=near[(p + 2) % 3][way], device_id_type=MESH
        )

    def mid_direct(p, way):
        d = 1 + 2 * way
        return remote(p, way, buf["msend"][p].at[pl.ds((d - 1) * cap, cap)],
                      buf["mrecv"][p].at[pl.ds(d * cap, cap)], m_send, m_recv)

    def mid_transit(p, way):
        return remote(p, way, buf["msend"][p].at[pl.ds(cap + way * half, half)],
                      buf["mtrans"][p].at[way], mt_send, mt_recv)

    def mid_forward(p, way):
        return remote(p, way, buf["mtrans"][p].at[way],
                      buf["mrecv"][p].at[pl.ds(2 * cap + way * half, half)], mf_send, mf_recv)

    def far(p, way):
        return remote3(p, way, buf["psend"][p].at[pl.ds(32 + 8 * way, 8)], buf["rtrans"][p].at[way], rt_send, rt_recv)

    def near_now(p, way):
        d = 1 + 2 * way
        part = 8 * (1 - way)
        return remote3(p, way, buf["psend"][p].at[pl.ds(16 * d + part, 8)],
                       buf["rrecv"][p].at[way, pl.ds(part, 8)], r0_send, r0_recv)

    def near_late(p, way):
        d = 1 + 2 * way
        part = 8 * way
        return remote3(p, way, buf["psend"][p].at[pl.ds(16 * d + part, 8)],
                       buf["rrecv"][p].at[way, pl.ds(part, 8)], r1_send, r1_recv)

    for p in range(3):
        load(p).start()
    greet([d for pair in near for d in pair])
    prefix[total] = jnp.zeros(prefix.shape[1:], BF16)

    def fill(p, d):
        def body(j, carry):
            index = table[first + p * total + d * cap + j]
            value = buf["gath"][p][index]
            if d == 0:
                buf["mrecv"][p][j] = value
            else:
                buf["msend"][p][(d - 1) * cap + j] = value
            return carry

        lax.fori_loop(0, cap, body, 0)

    for p in range(3):
        load(p).wait()
        fill(p, 2)
        mid_transit(p, 0).start()
        mid_transit(p, 1).start()
    for p in range(3):
        fill(p, 1)
        mid_direct(p, 0).start()
        fill(p, 3)
        mid_direct(p, 1).start()
    for p in range(3):
        for way in range(2):
            mid_transit(p, way).wait_recv()
            mid_forward(p, way).start()
    for p in range(3):
        fill(p, 0)

    for p in range(3):
        size = PARTS[p][1]
        for way in range(2):
            mid_direct(p, way).wait_recv()
            mid_forward(p, way).wait_recv()

        def run(n, acc, p=p, size=size):
            value = buf["mrecv"][p][table[order + p * total + n]].astype(F32)
            acc = acc * table[keep + p * total + n].astype(F32) + value
            prefix[n, pl.ds(0, size)] = acc.astype(BF16)
            return acc

        lax.fori_loop(0, total, run, jnp.zeros((size, 128), F32))

        def rows(d, p=p, size=size):
            def body(r, carry):
                index = table[last + p * 64 + d * 16 + r]
                buf["psend"][p][d * 16 + r] = prefix[index, pl.ds(0, size)]
                return carry

            lax.fori_loop(0, ROWS_DEV, body, 0)

        rows(2)
        far(p, 0).start()
        far(p, 1).start()
        rows(1)
        near_now(p, 0).start()
        rows(3)
        near_now(p, 1).start()
        rows(0)

    for p in range(3):
        for way in range(2):
            far(p, way).wait_recv()
            base = 16 * (1 + 2 * way) + 8 * way

            def add(r, carry, p=p, way=way, base=base):
                buf["psend"][p][base + r] = (
                    buf["psend"][p][base + r].astype(F32) + buf["rtrans"][p][way, r].astype(F32)
                ).astype(BF16)
                return carry

            lax.fori_loop(0, 8, add, 0)
            near_late(p, way).start()
    for p in range(3):
        for way in range(2):
            near_now(p, way).wait_recv()
            near_late(p, way).wait_recv()

        def final(r, carry, p=p):
            out_ref[r, pl.ds(*PARTS[p])] = (
                buf["psend"][p][r].astype(F32)
                + buf["rrecv"][p][0, r].astype(F32)
                + buf["rrecv"][p][1, r].astype(F32)
            ).astype(BF16)
            return carry

        lax.fori_loop(0, ROWS_DEV, final, 0)
    for p in range(3):
        for way in range(2):
            mid_direct(p, way).wait_send()
            mid_transit(p, way).wait_send()
            mid_forward(p, way).wait_send()
            far(p, way).wait_send()
            near_now(p, way).wait_send()
            near_late(p, way).wait_send()


def route(cap, ident, gathered, table):
    items = gathered.shape[0]
    total = RING * cap
    sizes = [size for _, size in PARTS]
    dma = pltpu.SemaphoreType.DMA

    def per_part(*lead):
        return [pltpu.VMEM(lead + (size, 128), BF16) for size in sizes]

    return pl.pallas_call(
        functools.partial(route_kernel, cap),
        name="route%d" % cap,
        out_shape=jax.ShapeDtypeStruct((ROWS_DEV, HALF, 128), BF16),
        in_specs=[pl.BlockSpec(memory_space=pltpu.SMEM), pl.BlockSpec(memory_space=pl.ANY)],
        out_specs=pl.BlockSpec(memory_space=pltpu.VMEM),
        scratch_shapes=[pltpu.VMEM((total + 1, max(sizes), 128), BF16)]
        + per_part(items)
        + per_part(3 * cap)
        + per_part(total)
        + per_part(2, cap // 2)
        + per_part(64)
        + per_part(2, 8)
        + per_part(2, ROWS_DEV)
        + [dma((3,))]
        + [dma((3, 2))] * 12,
        compiler_params=pltpu.CompilerParams(
            collective_id=ident, has_side_effects=True, vmem_limit_bytes=60 * 2**20
        ),
        cost_estimate=pl.CostEstimate(flops=10**7, bytes_accessed=10**7, transcendentals=0),
    )(table, gathered)


def part_axes(p):
    return p, (p + 1) % 3, (p + 2) % 3


def plane_items(listing):
    me = lax.axis_index("ctx")
    coords = [(me // s) % RING for s in STRIDES]
    ring = jnp.arange(RING)
    picks = []
    for p in range(3):
        a1, a2, a3 = part_axes(p)
        one = jnp.mod(coords[a1] - ring, RING) * STRIDES[a1]
        two = jnp.mod(coords[a2] - ring, RING) * STRIDES[a2]
        picks.append(two[:, None] + one[None, :] + coords[a3] * STRIDES[a3])
    return listing[jnp.stack(picks)].reshape(3, RING, -1), coords


def owner_coords(codes):
    owner = codes // ROWS_DEV
    return [(owner // s) % RING for s in STRIDES]


def most_slots(listing):
    own = owner_coords(listing.reshape(RING, RING, RING, -1))
    most = 0
    classes = jnp.arange(RING * RING)
    for p in range(3):
        a1, a2, _ = part_axes(p)
        label = own[a1] * RING + own[a2]
        hits = (label[..., None] == classes).astype(jnp.int32)
        most = jnp.maximum(most, jnp.max(jnp.sum(hits, axis=(p, 3))))
    return most


def tables(listing, cap):
    total = RING * cap
    codes, coords = plane_items(listing)
    own = owner_coords(codes)
    axes = [part_axes(p) for p in range(3)]

    def along(which):
        values = jnp.stack([own[axes[p][which]][p] for p in range(3)])
        mine = jnp.stack([coords[axes[p][which]] for p in range(3)])
        return values, mine

    o1, m1 = along(0)
    o2, m2 = along(1)
    o3, m3 = along(2)
    entries = codes.shape[-1]
    entry = jnp.arange(entries)
    line_rel = o1[:, 0] == m1[:, None]
    line_d = jnp.mod(o2[:, 0] - m2[:, None], RING)
    earlier = entry[None, :] < entry[:, None]
    rank = jnp.sum(
        (line_rel[:, None, :] & (line_d[:, None, :] == line_d[:, :, None]) & earlier).astype(jnp.int32), axis=-1
    )
    slot = jnp.where(line_rel, line_d * cap + rank, -1)
    send = jnp.sum(jnp.where(slot[:, None, :] == jnp.arange(total)[None, :, None], entry, 0), axis=-1)
    rel = (o1 == m1[:, None, None]) & (o2 == m2[:, None, None])
    got = jnp.sum((rel[:, :, None, :] & earlier).astype(jnp.int32), axis=-1)
    place = (jnp.arange(RING)[None, :, None] * cap + got).reshape(3, -1)
    key = (jnp.mod(o3 - m3[:, None, None], RING) * ROWS_DEV + codes % ROWS_DEV).reshape(3, -1)
    rel = rel.reshape(3, -1)
    key = jnp.where(rel, key, 64)
    full = jnp.where(rel, key * total + place, 64 * total)
    pos = jnp.sum((full[:, None, :] < full[:, :, None]).astype(jnp.int32), axis=-1)
    follows = jnp.any((key[:, None, :] == key[:, :, None]) & (place[:, None, :] < place[:, :, None]), axis=-1)
    at = (pos[:, None, :] == jnp.arange(total)[None, :, None]) & rel[:, None, :]
    order = jnp.sum(jnp.where(at, place[:, None, :], 0), axis=-1)
    keep = jnp.sum(jnp.where(at, follows[:, None, :].astype(jnp.int32), 0), axis=-1)
    wanted = jnp.arange(64)[None, :, None]
    below = jnp.sum((key[:, None, :] <= wanted).astype(jnp.int32), axis=-1)
    exists = jnp.any(key[:, None, :] == wanted, axis=-1)
    last = jnp.where(exists, below - 1, total)
    return jnp.concatenate([send.reshape(-1), order.reshape(-1), keep.reshape(-1), last.reshape(-1)])


def local(queries, nb_kv, out_grad, kv_weight, nb_owner, nb_row):
    codes = (nb_owner * ROWS_DEV + nb_row).reshape(1, -1)
    listing = lax.all_gather(codes, "ctx", axis=0, tiled=True)
    input_grad, gathered = relay(queries[0], nb_kv[0], out_grad, kv_weight[0])
    gathered = gathered.reshape(-1, HALF, 128)
    worst = RING * RING * CAP
    few = worst // 2
    fits = most_slots(listing) <= few
    packed = lax.cond(
        fits,
        lambda g: route(few, 1, g, tables(listing, few)),
        lambda g: route(worst, 2, g, tables(listing, worst)),
        gathered,
    )
    wide = packed[:, :384].reshape(ROWS_DEV, 3, NBLEN, 128).transpose(0, 2, 1, 3).reshape(ROWS_DEV, NBLEN, 384)
    tail = packed[:, 384:].reshape(ROWS_DEV, 64, 2, 64).transpose(0, 2, 1, 3).reshape(ROWS_DEV, NBLEN, 64)
    enc = jnp.concatenate([wide, tail], axis=-1)
    return (input_grad.reshape(queries.shape), enc)


def solution(mesh):
    in_specs = (
        P("section", "ctx", None),
        P("section", "ctx", None, None, None),
        P("ctx", None),
        P("section", None, None),
        P("ctx", None),
        P("ctx", None),
    )
    out_specs = (P("section", "ctx", None), P("ctx", None, "section"))
    return jax.shard_map(local, mesh=mesh, in_specs=in_specs, out_specs=out_specs, check_vma=False)
```

```python
import functools
import math

import jax
import jax.numpy as jnp
from jax import lax
from jax.experimental import pallas as pl
from jax.experimental.pallas import tpu as pltpu
from jax.sharding import PartitionSpec as P

HEADS = 16
KV_HEADS = 4
GROUP = HEADS // KV_HEADS
HDIM = 128
SPAN = 64
NB = 2
NBLEN = 128
CAP = 2
RING = 4
ROWS_DEV = 16
STRIDES = (16, 4, 1)
HALF = 448
PARTS = ((0, 160), (160, 144), (304, 144))
LAG_SUM = 2
LAG_FWD = 4
F32 = jnp.float32
BF16 = jnp.bfloat16
MESH = pl.DeviceIdType.MESH


def axis_step(axis, delta):
    me = lax.axis_index("ctx")
    stride = STRIDES[axis]
    coord = lax.rem(me // stride, RING)
    return me + (lax.rem(coord + delta + RING, RING) - coord) * stride


def greet(devices):
    barrier = pltpu.get_barrier_semaphore()
    for device in devices:
        pl.semaphore_signal(barrier, inc=1, device_id=device, device_id_type=MESH)
    pl.semaphore_wait(barrier, len(devices))


def neighbours():
    sec = lax.axis_index("section")
    return [[(sec, axis_step(a, 1)), (sec, axis_step(a, -1))] for a in range(3)]


def nt(a, b):
    return lax.dot_general(a, b, (((1,), (1,)), ((), ())), preferred_element_type=F32)


def nn(a, b):
    return lax.dot_general(a, b, (((1,), (0,)), ((), ())), preferred_element_type=F32)


def tn(a, b):
    return lax.dot_general(a, b, (((0,), (0,)), ((), ())), preferred_element_type=F32)


def relay_kernel(
    q_hbm, kv_hbm, og_hbm, w_hbm, code_hbm, ig_hbm, gath_hbm, list_hbm,
    q_v, kv_v, cot_v, ig_v, w_v, kvg_v, own_v, xsend_v, xrecv_v, gown_v,
    ld_sem, w_sem, out_sem, cs_send, cs_recv, xs_send, xs_recv, gl_sem,
    ag_send, ag_recv, fw_send, fw_recv, ls_sem, ls_send, ls_recv,
):
    spans = kv_v.shape[0]
    sec = lax.axis_index("section")
    me = lax.axis_index("ctx")
    partner = (1 - sec, me)
    near = neighbours()
    scale = 1.0 / math.sqrt(HDIM)

    def load(c, which):
        hbm, vmem = ((q_hbm, q_v), (kv_hbm, kv_v), (og_hbm, cot_v))[which]
        return pltpu.make_async_copy(hbm.at[c], vmem.at[c], ld_sem.at[c, which])

    def load_w():
        return pltpu.make_async_copy(w_hbm, w_v, w_sem)

    def list_own():
        return pltpu.make_async_copy(code_hbm, list_hbm.at[0, 0, 0], ls_sem)

    def list_copy(stage, hop):
        view = (lambda k: list_hbm.at[0, 0, k], lambda k: list_hbm.at[0, k], lambda k: list_hbm.at[k])[stage]
        source, target = ((0, 1), (0, 3), (1, 2))[hop]
        return pltpu.make_async_remote_copy(
            view(source), view(target), ls_send.at[stage, hop], ls_recv.at[stage, hop],
            device_id=near[2 - stage][hop % 2], device_id_type=MESH,
        )

    def out_copy(c):
        return pltpu.make_async_copy(ig_v.at[c], ig_hbm.at[c], out_sem.at[c])

    def cot_copy(c):
        return pltpu.make_async_remote_copy(
            ig_v.at[c], cot_v.at[c], cs_send.at[c], cs_recv.at[c], device_id=partner, device_id_type=MESH
        )

    def proj_copy(c):
        return pltpu.make_async_remote_copy(
            xsend_v.at[c], xrecv_v.at[c], xs_send.at[c], xs_recv.at[c], device_id=partner, device_id_type=MESH
        )

    def own_copy(c):
        return pltpu.make_async_copy(gown_v.at[c], gath_hbm.at[0, c], gl_sem.at[c])

    def gather_copy(c, p, way):
        rows = pl.ds(*PARTS[p])
        return pltpu.make_async_remote_copy(
            gown_v.at[c, :, rows], gath_hbm.at[1 + 2 * way, c, :, rows],
            ag_send.at[c, p, way], ag_recv.at[c, p, way], device_id=near[p][way], device_id_type=MESH,
        )

    def forward_copy(c, p, way):
        rows = pl.ds(*PARTS[p])
        return pltpu.make_async_remote_copy(
            gath_hbm.at[1 + 2 * way, c, way, rows], gath_hbm.at[2, c, way, rows],
            fw_send.at[c, p, way], fw_recv.at[c, p, way], device_id=near[p][way], device_id_type=MESH,
        )

    def start_loads(c, carry):
        load(c, 0).start()
        load(c, 1).start()

        @pl.when(sec == 1)
        def _():
            load(c, 2).start()

        return carry

    lax.fori_loop(0, 1, start_loads, 0)
    load_w().start()
    list_own().start()
    lax.fori_loop(1, spans, start_loads, 0)

    greet([partner] + [d for pair in near for d in pair])

    list_own().wait()
    list_copy(0, 0).start()
    list_copy(0, 1).start()
    load_w().wait()

    def attend(c):
        for h in range(KV_HEADS):
            heads = [slice((h * GROUP + g) * HDIM, (h * GROUP + g + 1) * HDIM) for g in range(GROUP)]
            cols = slice(h * HDIM, (h + 1) * HDIM)
            vcols = slice((KV_HEADS + h) * HDIM, (KV_HEADS + h + 1) * HDIM)
            q = jnp.concatenate([q_v[c, :, s] for s in heads], axis=0)
            g = jnp.concatenate([cot_v[c, :, s] for s in heads], axis=0)
            k = kv_v[c, :, cols]
            v = kv_v[c, :, vcols]
            s = nt(k, q) * (scale * math.log2(math.e))
            e = jnp.exp2(s - jnp.max(s, axis=0, keepdims=True))
            prob = e * (1.0 / jnp.sum(e, axis=0, keepdims=True))
            low = prob.astype(BF16)
            dp = nt(v, g)
            dot = jnp.sum(low.astype(F32) * dp, axis=0, keepdims=True)
            ds = (prob * (dp - dot)).astype(BF16)
            kvg_v[:, vcols] = nn(low, g).astype(BF16)
            kvg_v[:, cols] = (nn(ds, q) * scale).astype(BF16)
            grad = (g.astype(F32) + tn(ds, k) * scale).astype(BF16)
            for i, col in enumerate(heads):
                ig_v[c, :, col] = grad[i * SPAN : (i + 1) * SPAN]

    def project(c):
        kvg = kvg_v[...]
        other = nt(w_v[1 - sec], kvg)
        for n in range(NB):
            xsend_v[c, n] = other[:, n * NBLEN : (n + 1) * NBLEN].astype(BF16)
        proj_copy(c).start()
        mine = nt(w_v[sec], kvg)
        for n in range(NB):
            own_v[c, n] = mine[:, n * NBLEN : (n + 1) * NBLEN]

    def spread_lists(t):
        for stage in range(3):

            @pl.when(t == 2 * stage + 1)
            def _(stage=stage):
                list_copy(stage, 0).wait_recv()
                list_copy(stage, 2).start()

            @pl.when(t == 2 * stage + 2)
            def _(stage=stage):
                list_copy(stage, 1).wait_recv()
                list_copy(stage, 2).wait_recv()
                if stage < 2:
                    list_copy(stage + 1, 0).start()
                    list_copy(stage + 1, 1).start()

    def step(t, carry):
        c = t - (1 - sec)
        live = (c >= 0) & (c < spans)

        @pl.when(live)
        def _():
            load(c, 0).wait()
            load(c, 1).wait()

            @pl.when(sec == 1)
            def _():
                load(c, 2).wait()

            @pl.when(sec == 0)
            def _():
                cot_copy(c).wait_recv()

            attend(c)
            out_copy(c).start()

            @pl.when(sec == 1)
            def _():
                cot_copy(c).start()

        spread_lists(t)
        s = t - LAG_SUM

        @pl.when((s >= 0) & (s < spans))
        def _():
            proj_copy(s).wait_recv()
            for n in range(NB):
                gown_v[s, n] = (own_v[s, n] + xrecv_v[s, n].astype(F32)).astype(BF16)
            for p in range(3):
                for way in range(2):
                    gather_copy(s, p, way).start()
            own_copy(s).start()

        f = t - LAG_FWD

        @pl.when((f >= 0) & (f < spans))
        def _():
            for p in range(3):
                for way in range(2):
                    gather_copy(f, p, way).wait_recv()
                    forward_copy(f, p, way).start()

        @pl.when(live)
        def _():
            project(c)

        return carry

    lax.fori_loop(0, spans + LAG_FWD, step, 0)

    def finish(c, carry):
        out_copy(c).wait()

        @pl.when(sec == 1)
        def _():
            cot_copy(c).wait_send()

        proj_copy(c).wait_send()
        own_copy(c).wait()
        for p in range(3):
            for way in range(2):
                gather_copy(c, p, way).wait_send()
                forward_copy(c, p, way).wait()
        return carry

    lax.fori_loop(0, spans, finish, 0)
    for stage in range(3):
        for hop in range(3):
            list_copy(stage, hop).wait_send()


def relay(queries, nb_kv, out_grad, weight, codes):
    spans = nb_kv.shape[0]
    kvw2 = nb_kv.shape[-1]
    inner = queries.shape[-1]
    dma = pltpu.SemaphoreType.DMA
    item = (spans, NB, HALF, 128)
    any_spec = pl.BlockSpec(memory_space=pl.ANY)
    return pl.pallas_call(
        relay_kernel,
        name="relay",
        out_shape=(
            jax.ShapeDtypeStruct((spans, SPAN, inner), BF16),
            jax.ShapeDtypeStruct((RING,) + item, BF16),
            jax.ShapeDtypeStruct((RING, RING, RING, 1, 128), jnp.int32),
        ),
        in_specs=[any_spec] * 5,
        out_specs=(any_spec,) * 3,
        scratch_shapes=[
            pltpu.VMEM((spans, SPAN, inner), BF16),
            pltpu.VMEM((spans, NB * NBLEN, kvw2), BF16),
            pltpu.VMEM((spans, SPAN, inner), BF16),
            pltpu.VMEM((spans, SPAN, inner), BF16),
            pltpu.VMEM((2, HALF, kvw2), BF16),
            pltpu.VMEM((NB * NBLEN, kvw2), BF16),
            pltpu.VMEM(item, F32),
            pltpu.VMEM(item, BF16),
            pltpu.VMEM(item, BF16),
            pltpu.VMEM(item, BF16),
            dma((spans, 3)),
            dma(()),
            dma((spans,)),
            dma((spans,)),
            dma((spans,)),
            dma((spans,)),
            dma((spans,)),
            dma((spans,)),
            dma((spans, 3, 2)),
            dma((spans, 3, 2)),
            dma((spans, 3, 2)),
            dma((spans, 3, 2)),
            dma(()),
            dma((3, 3)),
            dma((3, 3)),
        ],
        compiler_params=pltpu.CompilerParams(
            collective_id=0, has_side_effects=True, vmem_limit_bytes=60 * 2**20
        ),
        cost_estimate=pl.CostEstimate(flops=7 * 10**9, bytes_accessed=20 * 10**6, transcendentals=2**21),
    )(
        queries.reshape(spans, SPAN, inner),
        nb_kv.reshape(spans, NB * NBLEN, kvw2),
        out_grad.reshape(spans, SPAN, inner),
        weight.reshape(2, HALF, kvw2),
        codes,
    )


def route_kernel(cap, table, gath_hbm, out_ref, prefix, *refs):
    names = ("gath", "msend", "mrecv", "mtrans", "psend", "rtrans", "rrecv")
    buf = {name: refs[3 * i : 3 * i + 3] for i, name in enumerate(names)}
    (ld_sem, m_send, m_recv, mt_send, mt_recv, mf_send, mf_recv,
     rt_send, rt_recv, r0_send, r0_recv, r1_send, r1_recv) = refs[3 * len(names) :]
    total = RING * cap
    half = cap // 2
    near = neighbours()
    first, order, keep, last = 0, 3 * total, 6 * total, 9 * total

    def load(p):
        return pltpu.make_async_copy(gath_hbm.at[:, pl.ds(*PARTS[p])], buf["gath"][p], ld_sem.at[p])

    def remote(p, way, src, dst, send, recv):
        return pltpu.make_async_remote_copy(
            src, dst, send.at[p, way], recv.at[p, way], device_id=near[(p + 1) % 3][way], device_id_type=MESH
        )

    def remote3(p, way, src, dst, send, recv):
        return pltpu.make_async_remote_copy(
            src, dst, send.at[p, way], recv.at[p, way], device_id=near[(p + 2) % 3][way], device_id_type=MESH
        )

    def mid_direct(p, way):
        d = 1 + 2 * way
        return remote(p, way, buf["msend"][p].at[pl.ds((d - 1) * cap, cap)],
                      buf["mrecv"][p].at[pl.ds(d * cap, cap)], m_send, m_recv)

    def mid_transit(p, way):
        return remote(p, way, buf["msend"][p].at[pl.ds(cap + way * half, half)],
                      buf["mtrans"][p].at[way], mt_send, mt_recv)

    def mid_forward(p, way):
        return remote(p, way, buf["mtrans"][p].at[way],
                      buf["mrecv"][p].at[pl.ds(2 * cap + way * half, half)], mf_send, mf_recv)

    def far(p, way):
        return remote3(p, way, buf["psend"][p].at[pl.ds(32 + 8 * way, 8)], buf["rtrans"][p].at[way], rt_send, rt_recv)

    def near_now(p, way):
        d = 1 + 2 * way
        part = 8 * (1 - way)
        return remote3(p, way, buf["psend"][p].at[pl.ds(16 * d + part, 8)],
                       buf["rrecv"][p].at[way, pl.ds(part, 8)], r0_send, r0_recv)

    def near_late(p, way):
        d = 1 + 2 * way
        part = 8 * way
        return remote3(p, way, buf["psend"][p].at[pl.ds(16 * d + part, 8)],
                       buf["rrecv"][p].at[way, pl.ds(part, 8)], r1_send, r1_recv)

    for p in range(3):
        load(p).start()
    greet([d for pair in near for d in pair])
    prefix[total] = jnp.zeros(prefix.shape[1:], BF16)

    def fill(p, d):
        def body(j, carry):
            index = table[first + p * total + d * cap + j]
            value = buf["gath"][p][index]
            if d == 0:
                buf["mrecv"][p][j] = value
            else:
                buf["msend"][p][(d - 1) * cap + j] = value
            return carry

        lax.fori_loop(0, cap, body, 0)

    for p in range(3):
        load(p).wait()
        fill(p, 2)
        mid_transit(p, 0).start()
        mid_transit(p, 1).start()
    for p in range(3):
        fill(p, 1)
        mid_direct(p, 0).start()
        fill(p, 3)
        mid_direct(p, 1).start()
    for p in range(3):
        for way in range(2):
            mid_transit(p, way).wait_recv()
            mid_forward(p, way).start()
    for p in range(3):
        fill(p, 0)

    for p in range(3):
        size = PARTS[p][1]
        for way in range(2):
            mid_direct(p, way).wait_recv()
            mid_forward(p, way).wait_recv()

        def run(n, acc, p=p, size=size):
            value = buf["mrecv"][p][table[order + p * total + n]].astype(F32)
            acc = acc * table[keep + p * total + n].astype(F32) + value
            prefix[n, pl.ds(0, size)] = acc.astype(BF16)
            return acc

        lax.fori_loop(0, total, run, jnp.zeros((size, 128), F32))

        def rows(d, p=p, size=size):
            def body(r, carry):
                index = table[last + p * 64 + d * 16 + r]
                buf["psend"][p][d * 16 + r] = prefix[index, pl.ds(0, size)]
                return carry

            lax.fori_loop(0, ROWS_DEV, body, 0)

        rows(2)
        far(p, 0).start()
        far(p, 1).start()
        rows(1)
        near_now(p, 0).start()
        rows(3)
        near_now(p, 1).start()
        rows(0)

    for p in range(3):
        for way in range(2):
            far(p, way).wait_recv()
            base = 16 * (1 + 2 * way) + 8 * way

            def add(r, carry, p=p, way=way, base=base):
                buf["psend"][p][base + r] = (
                    buf["psend"][p][base + r].astype(F32) + buf["rtrans"][p][way, r].astype(F32)
                ).astype(BF16)
                return carry

            lax.fori_loop(0, 8, add, 0)
            near_late(p, way).start()
    for p in range(3):
        for way in range(2):
            near_now(p, way).wait_recv()
            near_late(p, way).wait_recv()

        def final(r, carry, p=p):
            out_ref[r, pl.ds(*PARTS[p])] = (
                buf["psend"][p][r].astype(F32)
                + buf["rrecv"][p][0, r].astype(F32)
                + buf["rrecv"][p][1, r].astype(F32)
            ).astype(BF16)
            return carry

        lax.fori_loop(0, ROWS_DEV, final, 0)
    for p in range(3):
        for way in range(2):
            mid_direct(p, way).wait_send()
            mid_transit(p, way).wait_send()
            mid_forward(p, way).wait_send()
            far(p, way).wait_send()
            near_now(p, way).wait_send()
            near_late(p, way).wait_send()


def route(cap, ident, gathered, table):
    items = gathered.shape[0]
    total = RING * cap
    sizes = [size for _, size in PARTS]
    dma = pltpu.SemaphoreType.DMA

    def per_part(*lead):
        return [pltpu.VMEM(lead + (size, 128), BF16) for size in sizes]

    return pl.pallas_call(
        functools.partial(route_kernel, cap),
        name="route%d" % cap,
        out_shape=jax.ShapeDtypeStruct((ROWS_DEV, HALF, 128), BF16),
        in_specs=[pl.BlockSpec(memory_space=pltpu.SMEM), pl.BlockSpec(memory_space=pl.ANY)],
        out_specs=pl.BlockSpec(memory_space=pltpu.VMEM),
        scratch_shapes=[pltpu.VMEM((total + 1, max(sizes), 128), BF16)]
        + per_part(items)
        + per_part(3 * cap)
        + per_part(total)
        + per_part(2, cap // 2)
        + per_part(64)
        + per_part(2, 8)
        + per_part(2, ROWS_DEV)
        + [dma((3,))]
        + [dma((3, 2))] * 12,
        compiler_params=pltpu.CompilerParams(
            collective_id=ident, has_side_effects=True, vmem_limit_bytes=60 * 2**20
        ),
        cost_estimate=pl.CostEstimate(flops=10**7, bytes_accessed=10**7, transcendentals=0),
    )(table, gathered)


def part_axes(p):
    return p, (p + 1) % 3, (p + 2) % 3


def plane_items(listing):
    me = lax.axis_index("ctx")
    coords = [(me // s) % RING for s in STRIDES]
    planes = [listing[:, :, 0].swapaxes(0, 1), listing[0].swapaxes(0, 1), listing[:, 0]]
    return jnp.stack(planes).reshape(3, RING, -1), coords


def owner_coords(codes):
    owner = codes // ROWS_DEV
    return [(owner // s) % RING for s in STRIDES]


def most_slots(listing):
    own = owner_coords(listing)
    most = 0
    classes = jnp.arange(RING * RING)
    for p in range(3):
        a1, a2, _ = part_axes(p)
        label = own[a1] * RING + own[a2]
        hits = (label[..., None] == classes).astype(jnp.int32)
        most = jnp.maximum(most, jnp.max(jnp.sum(hits, axis=(p, 3))))
    return most


def tables(listing, cap):
    total = RING * cap
    codes, coords = plane_items(listing)
    own = owner_coords(codes)
    axes = [part_axes(p) for p in range(3)]

    def along(which):
        values = jnp.stack([own[axes[p][which]][p] for p in range(3)])
        mine = jnp.stack([coords[axes[p][which]] for p in range(3)])
        return values, mine

    o1, m1 = along(0)
    o2, m2 = along(1)
    o3, m3 = along(2)
    entries = codes.shape[-1]
    entry = jnp.arange(entries)
    line_rel = o1[:, 0] == m1[:, None]
    line_d = jnp.mod(o2[:, 0] - m2[:, None], RING)
    earlier = entry[None, :] < entry[:, None]
    rank = jnp.sum(
        (line_rel[:, None, :] & (line_d[:, None, :] == line_d[:, :, None]) & earlier).astype(jnp.int32), axis=-1
    )
    slot = jnp.where(line_rel, line_d * cap + rank, -1)
    send = jnp.sum(jnp.where(slot[:, None, :] == jnp.arange(total)[None, :, None], entry, 0), axis=-1)
    rel = (o1 == m1[:, None, None]) & (o2 == m2[:, None, None])
    got = jnp.sum((rel[:, :, None, :] & earlier).astype(jnp.int32), axis=-1)
    place = (jnp.arange(RING)[None, :, None] * cap + got).reshape(3, -1)
    key = (jnp.mod(o3 - m3[:, None, None], RING) * ROWS_DEV + codes % ROWS_DEV).reshape(3, -1)
    rel = rel.reshape(3, -1)
    key = jnp.where(rel, key, 64)
    full = jnp.where(rel, key * total + place, 64 * total)
    pos = jnp.sum((full[:, None, :] < full[:, :, None]).astype(jnp.int32), axis=-1)
    follows = jnp.any((key[:, None, :] == key[:, :, None]) & (place[:, None, :] < place[:, :, None]), axis=-1)
    at = (pos[:, None, :] == jnp.arange(total)[None, :, None]) & rel[:, None, :]
    order = jnp.sum(jnp.where(at, place[:, None, :], 0), axis=-1)
    keep = jnp.sum(jnp.where(at, follows[:, None, :].astype(jnp.int32), 0), axis=-1)
    wanted = jnp.arange(64)[None, :, None]
    below = jnp.sum((key[:, None, :] <= wanted).astype(jnp.int32), axis=-1)
    exists = jnp.any(key[:, None, :] == wanted, axis=-1)
    last = jnp.where(exists, below - 1, total)
    return jnp.concatenate([send.reshape(-1), order.reshape(-1), keep.reshape(-1), last.reshape(-1)])


def local(queries, nb_kv, out_grad, kv_weight, nb_owner, nb_row):
    codes = (nb_owner * ROWS_DEV + nb_row).reshape(1, -1)
    entries = codes.shape[-1]
    codes = jnp.pad(codes, ((0, 0), (0, 128 - entries)))
    input_grad, gathered, listing = relay(queries[0], nb_kv[0], out_grad, kv_weight[0], codes)
    listing = listing[..., 0, :entries]
    gathered = gathered.reshape(-1, HALF, 128)
    worst = RING * RING * CAP
    few = worst // 2
    fits = most_slots(listing) <= few
    packed = lax.cond(
        fits,
        lambda g: route(few, 1, g, tables(listing, few)),
        lambda g: route(worst, 2, g, tables(listing, worst)),
        gathered,
    )
    return (input_grad.reshape(queries.shape), packed.swapaxes(1, 2))


def solution(mesh):
    in_specs = (
        P("section", "ctx", None),
        P("section", "ctx", None, None, None),
        P("ctx", None),
        P("section", None, None),
        P("ctx", None),
        P("ctx", None),
    )
    out_specs = (P("section", "ctx", None), P("ctx", None, "section"))
    return jax.shard_map(local, mesh=mesh, in_specs=in_specs, out_specs=out_specs, check_vma=False)
```

```python
import functools
import math

import jax
import jax.numpy as jnp
from jax import lax
from jax.experimental import pallas as pl
from jax.experimental.pallas import tpu as pltpu
from jax.sharding import PartitionSpec as P

HEADS = 16
KV_HEADS = 4
GROUP = HEADS // KV_HEADS
HDIM = 128
SPAN = 64
NB = 2
NBLEN = 128
CAP = 2
RING = 4
ROWS_DEV = 16
STRIDES = (16, 4, 1)
HALF = 448
PARTS = ((0, 160), (160, 144), (304, 144))
PIECES = ((0, 0, 80), (1, 160, 80), (2, 304, 80), (0, 80, 80), (1, 240, 64), (2, 384, 64))
FAST = (16, 16, 8)
FULL = (RING * RING * CAP,) * 3
LAG_SUM = 2
LAG_FWD = 4
SHIFTS = (4, 2, 0)
F32 = jnp.float32
BF16 = jnp.bfloat16
MESH = pl.DeviceIdType.MESH


def axis_step(axis, delta):
    me = lax.axis_index("ctx")
    stride = STRIDES[axis]
    coord = lax.rem(me // stride, RING)
    return me + (lax.rem(coord + delta + RING, RING) - coord) * stride


def greet(devices):
    barrier = pltpu.get_barrier_semaphore()
    for device in devices:
        pl.semaphore_signal(barrier, inc=1, device_id=device, device_id_type=MESH)
    pl.semaphore_wait(barrier, len(devices))


def neighbours():
    sec = lax.axis_index("section")
    return [[(sec, axis_step(a, 1)), (sec, axis_step(a, -1))] for a in range(3)]


def nt(a, b):
    return lax.dot_general(a, b, (((1,), (1,)), ((), ())), preferred_element_type=F32)


def nn(a, b):
    return lax.dot_general(a, b, (((1,), (0,)), ((), ())), preferred_element_type=F32)


def tn(a, b):
    return lax.dot_general(a, b, (((0,), (0,)), ((), ())), preferred_element_type=F32)


def part_axes(p):
    return p, (p + 1) % 3, (p + 2) % 3


def flags(mask):
    return jnp.where(mask, 1.0, 0.0).astype(BF16)


def count(mask, axis):
    return jnp.sum(jnp.where(mask, 1, 0), axis=axis, keepdims=True)


def pick(mask, values):
    return jnp.sum(jnp.where(mask, values, 0), axis=0, keepdims=True)


def plan(list_v, table_ref, most_ref):
    me = lax.axis_index("ctx")
    coords = [lax.rem(me // s, RING) for s in STRIDES]
    codes = jnp.concatenate([list_v[:, 0, :], list_v[:, 1, :]], axis=0)
    owners = (codes >> 4).astype(F32).astype(BF16)
    places = (codes & 15).astype(F32).astype(BF16)

    def as_column(values, at_row, at_lane):
        lane = lax.broadcasted_iota(jnp.int32, (at_row.shape[0], 128), 1)
        rows = nn(flags(lane == at_row), values)
        return jnp.sum(jnp.where(lane == at_lane, rows, 0.0), axis=1, keepdims=True).astype(jnp.int32)

    def as_row(values, at_row, at_lane):
        sub = lax.broadcasted_iota(jnp.int32, (128, at_row.shape[1]), 0)
        columns = nn(values, flags(sub == at_lane))
        return jnp.sum(jnp.where(sub == at_row, columns, 0.0), axis=0, keepdims=True).astype(jnp.int32)

    def share(n1, n2, n3, cap):
        low, high = jnp.maximum(n2 + n3 - cap[1], 0), jnp.minimum(n2, cap[1] - n1)
        return jnp.minimum(jnp.maximum(n2 >> 1, low), high), low, high

    every = lax.broadcasted_iota(jnp.int32, (1, 1024), 1)
    device = every >> 4
    owner_all = as_row(owners, ((every >> 3) & 1) * 64 + device, every & 7)
    sub = lax.broadcasted_iota(jnp.int32, (32, 1024), 0)
    over = jnp.zeros((1, 1), jnp.int32)
    for p in range(3):
        a1, a2, a3 = part_axes(p)
        f1, f2, f3 = [SHIFTS[a] for a in (a1, a2, a3)]
        away = (((owner_all >> f2) & 3) - coords[a2] + ((device >> f2) & 3)) & 3
        label = away * 8 + ((owner_all >> f1) & 3)
        line = ((device >> f2) & 3) * 4 + ((device >> f3) & 3)
        hits = nt(flags(sub == label), flags(sub[0:16] == line)).astype(jnp.int32)
        n0, n1, n2, n3 = [hits[8 * d : 8 * d + 8] for d in range(4)]
        right, low, high = share(n1, n2, n3, FAST)
        bad = (n0 > FAST[0]) | (low > high) | (right > FAST[2]) | (n2 - right > FAST[2])
        bad = jnp.max(jnp.where(bad, 1, 0), axis=1, keepdims=True)
        over = jnp.maximum(over, jnp.max(bad, axis=0, keepdims=True))
    most_ref[0, 0] = jnp.max(over)

    number = lax.broadcasted_iota(jnp.int32, (1, 128), 1)
    col = lax.broadcasted_iota(jnp.int32, (256, 1), 0)
    row = lax.broadcasted_iota(jnp.int32, (1, 256), 1)
    same = row >> 6 == col >> 6
    item_c = (col & 48) | ((col & 7) * 2 + ((col >> 3) & 1))
    for p in range(3):
        a1, a2, a3 = part_axes(p)

        def both(values):
            found = []
            for e, form in ((col, as_column), (row, as_row)):
                at_row = ((e >> 3) & 1) * 64 + (e >> 6) * STRIDES[a2] + ((e >> 4) & 3) * STRIDES[a1]
                found.append(form(values, at_row, e & 7))
            return found

        (own_c, own_r), (place_c, place_r) = both(owners), both(places)

        def fields(own, spot, e):
            o1, o2, o3 = [(own >> SHIFTS[a]) & 3 for a in (a1, a2, a3)]
            away = jnp.where(o1 == coords[a1], (o2 - coords[a2] + (e >> 6)) & 3, RING)
            key = jnp.where(away == e >> 6, ((o3 - coords[a3]) & 3) * ROWS_DEV + spot, 64)
            return away, key

        away_c, key_c = fields(own_c, place_c, col)
        away_r, key_r = fields(own_r, place_r, row)
        rank_c = count(same & (away_r == away_c) & (row < col), 1)
        rank_r = count(same & (away_r == away_c) & (col < row), 0)
        many_c = [count(same & (away_r == d), 1) for d in (1, 2, 3)]
        many_r = [count(same & (away_c == d), 0) for d in (1, 2, 3)]
        below = count(key_c <= number, 0)
        present = count(key_c == number, 0)
        for which, cap in enumerate((FAST, FULL)):
            stay, slots, passed = cap
            base = which * 12 + p * 4

            def slot(away, rank, many, behind):
                right = share(*many, cap)[0]
                one = stay + right + rank
                three = stay + slots + many[1] - right + rank
                two = jnp.where(rank < right, behind[0] + rank, behind[1] + rank - right)
                return jnp.where(
                    away == 0, rank, jnp.where(away == 1, one, jnp.where(away == 2, two, three))
                )

            sent_c = jnp.where((away_c < RING) & (col < 64), slot(away_c, rank_c, many_c, (stay, stay + slots)), -1)
            table_ref[pl.ds(base, 1)] = pick(sent_c == number, item_c)
            far = (stay + 2 * slots, stay + 2 * slots + passed)
            spot_c = slot(away_c, rank_c, many_c, far)
            spot_r = slot(away_r, rank_r, many_r, far)
            full_c = key_c * 256 + spot_c
            full_r = key_r * 256 + spot_r
            ahead = (full_r < full_c) & (key_r < 64)
            pos_c = jnp.where(key_c < 64, count(ahead, 1), -1)
            follows_c = jnp.where(count(ahead & (key_r == key_c), 1) > 0, 1, 0)
            table_ref[pl.ds(base + 1, 1)] = pick(pos_c == number, spot_c)
            table_ref[pl.ds(base + 2, 1)] = pick(pos_c == number, follows_c)
            table_ref[pl.ds(base + 3, 1)] = jnp.where(present > 0, below - 1, RING * stay)


def relay_kernel(
    q_hbm, kv_hbm, og_hbm, w_hbm, owner_ref, row_ref, ig_hbm, gath_hbm, table_ref, most_ref,
    q_v, kv_v, cot_v, ig_v, w_v, kvg_v, xsend_v, xrecv_v, gown_v, list_v,
    ld_sem, w_sem, out_sem, cs_send, cot_sem, xs_send, xs_recv, gl_sem,
    ag_send, ag_recv, fw_send, fw_recv, ls_send, ls_recv,
):
    spans = kv_v.shape[0]
    sec = lax.axis_index("section")
    me = lax.axis_index("ctx")
    partner = (1 - sec, me)
    near = neighbours()
    scale = 1.0 / math.sqrt(HDIM)

    def load(c, which):
        hbm, vmem = ((q_hbm, q_v), (kv_hbm, kv_v))[which]
        return pltpu.make_async_copy(hbm.at[c], vmem.at[c], ld_sem.at[c, which])

    def cot_load(c):
        return pltpu.make_async_copy(og_hbm.at[c], cot_v.at[0, c], cot_sem.at[0, c])

    def cot_send(c):
        return pltpu.make_async_remote_copy(
            ig_v.at[c], cot_v.at[1 - sec, c], cs_send.at[c], cot_sem.at[1 - sec, c],
            device_id=partner, device_id_type=MESH,
        )

    def load_w():
        return pltpu.make_async_copy(w_hbm, w_v, w_sem)

    def list_copy(stage, hop):
        size = RING**stage
        source, target = ((0, 1), (0, 3), (1, 2))[hop]
        return pltpu.make_async_remote_copy(
            list_v.at[pl.ds(source * size, size)], list_v.at[pl.ds(target * size, size)],
            ls_send.at[stage, hop], ls_recv.at[stage, hop],
            device_id=near[2 - stage][hop % 2], device_id_type=MESH,
        )

    def out_copy(c):
        return pltpu.make_async_copy(ig_v.at[c], ig_hbm.at[c], out_sem.at[c])

    def proj_copy(c):
        return pltpu.make_async_remote_copy(
            xsend_v.at[c], xrecv_v.at[c], xs_send.at[c], xs_recv.at[c], device_id=partner, device_id_type=MESH
        )

    def own_copy(c):
        return pltpu.make_async_copy(gown_v.at[c], gath_hbm.at[0, c], gl_sem.at[c])

    def gather_copy(c, p, way):
        rows = pl.ds(*PARTS[p])
        return pltpu.make_async_remote_copy(
            gown_v.at[c, :, rows], gath_hbm.at[1 + 2 * way, c, :, rows],
            ag_send.at[c, p, way], ag_recv.at[c, p, way], device_id=near[p][way], device_id_type=MESH,
        )

    def forward_copy(c, p, way):
        rows = pl.ds(*PARTS[p])
        return pltpu.make_async_remote_copy(
            gath_hbm.at[1 + 2 * way, c, way, rows], gath_hbm.at[2, c, way, rows],
            fw_send.at[c, p, way], fw_recv.at[c, p, way], device_id=near[p][way], device_id_type=MESH,
        )

    def start_loads(c, carry):
        load(c, 0).start()
        load(c, 1).start()

        @pl.when(sec == 1)
        def _():
            cot_load(c).start()

        return carry

    lax.fori_loop(0, 1, start_loads, 0)
    load_w().start()
    lax.fori_loop(1, spans, start_loads, 0)
    list_v[0] = jnp.zeros((NB, 128), jnp.int32)
    list_v[0, :, 0:spans] = owner_ref[...] * ROWS_DEV + row_ref[...]

    greet([partner] + [d for pair in near for d in pair])
    list_copy(0, 0).start()
    list_copy(0, 1).start()

    def attend(c, slot):
        def names(h):
            heads = [slice((h * GROUP + g) * HDIM, (h * GROUP + g + 1) * HDIM) for g in range(GROUP)]
            return heads, slice(h * HDIM, (h + 1) * HDIM), slice((KV_HEADS + h) * HDIM, (KV_HEADS + h + 1) * HDIM)

        def front(h):
            heads, cols, vcols = names(h)
            q = jnp.concatenate([q_v[c, :, s] for s in heads], axis=0)
            k = kv_v[c, :, cols]
            v = kv_v[c, :, vcols]
            s = nt(k, q)
            g = jnp.concatenate([cot_v[0, c, :, s] for s in heads], axis=0)
            return q, g, k, s, nt(v, g)

        def middle(q, g, k, s, dp):
            peak = jnp.max(s, axis=0, keepdims=True)
            e = jnp.exp2((s - peak) * (scale * math.log2(math.e)))
            prob = e * (1.0 / jnp.sum(e, axis=0, keepdims=True))
            low = prob.astype(BF16)
            dot = jnp.sum(low.astype(F32) * dp, axis=0, keepdims=True)
            return q, g, k, low, (prob * (dp - dot)).astype(BF16)

        def back(h, q, g, k, low, ds):
            heads, cols, vcols = names(h)
            grad = (g.astype(F32) + tn(ds, k) * scale).astype(BF16)
            for i, col in enumerate(heads):
                ig_v[c, :, col] = grad[i * SPAN : (i + 1) * SPAN]
            kvg_v[slot, :, vcols] = nn(low, g).astype(BF16)
            kvg_v[slot, :, cols] = (nn(ds, q) * scale).astype(BF16)

        now = front(0)
        done = None
        for h in range(KV_HEADS):
            ahead = front(h + 1) if h + 1 < KV_HEADS else None
            ready = middle(*now)
            if done is not None:
                back(h - 1, *done)
            done, now = ready, ahead
        back(KV_HEADS - 1, *done)

    def spread_lists(t):
        for stage in range(3):

            @pl.when(t == 2 * stage)
            def _(stage=stage):
                list_copy(stage, 0).wait_recv()
                list_copy(stage, 2).start()

            @pl.when(t == 2 * stage + 1)
            def _(stage=stage):
                list_copy(stage, 1).wait_recv()
                list_copy(stage, 2).wait_recv()
                if stage < 2:
                    list_copy(stage + 1, 0).start()
                    list_copy(stage + 1, 1).start()

    def step(t, carry):
        c = t - (1 - sec)
        live = (c >= 0) & (c < spans)
        slot = lax.rem(c + 3, 3)

        @pl.when(live)
        def _():
            load(c, 0).wait()
            load(c, 1).wait()
            cot_load(c).wait()
            attend(c, slot)
            cot_send(c).start()
            out_copy(c).start()

            @pl.when(c == 0)
            def _():
                load_w().wait()

        s = t - LAG_SUM

        @pl.when((s >= 0) & (s < spans))
        def _():
            mine = nt(w_v[sec], kvg_v[lax.rem(s, 3)])
            proj_copy(s).wait_recv()
            for n in range(NB):
                gown_v[s, n] = (mine[:, n * NBLEN : (n + 1) * NBLEN] + xrecv_v[s, n].astype(F32)).astype(BF16)
            for p in range(3):
                for way in range(2):
                    gather_copy(s, p, way).start()
            own_copy(s).start()

        @pl.when(live)
        def _():
            other = nt(w_v[1 - sec], kvg_v[slot])
            for n in range(NB):
                xsend_v[c, n] = other[:, n * NBLEN : (n + 1) * NBLEN].astype(BF16)
            proj_copy(c).start()

        f = t - LAG_FWD

        @pl.when((f >= 0) & (f < spans))
        def _():
            for p in range(3):
                for way in range(2):
                    gather_copy(f, p, way).wait_recv()
                    forward_copy(f, p, way).start()

        spread_lists(t)

        @pl.when(t == spans + 1)
        def _():
            plan(list_v, table_ref, most_ref)

        return carry

    lax.fori_loop(0, spans + LAG_FWD, step, 0)

    def finish(c, carry):
        out_copy(c).wait()
        cot_send(c).wait_send()

        @pl.when(sec == 1)
        def _():
            pltpu.make_async_copy(og_hbm.at[c], cot_v.at[1, c], cot_sem.at[1, c]).wait()

        proj_copy(c).wait_send()
        own_copy(c).wait()
        for p in range(3):
            for way in range(2):
                gather_copy(c, p, way).wait_send()
                forward_copy(c, p, way).wait()
        return carry

    lax.fori_loop(0, spans, finish, 0)
    for stage in range(3):
        for hop in range(3):
            list_copy(stage, hop).wait_send()


def relay(queries, nb_kv, out_grad, weight, owners, rows):
    spans = nb_kv.shape[0]
    kvw2 = nb_kv.shape[-1]
    inner = queries.shape[-1]
    dma = pltpu.SemaphoreType.DMA
    item = (spans, NB, HALF, 128)
    any_spec = pl.BlockSpec(memory_space=pl.ANY)
    vmem_spec = pl.BlockSpec(memory_space=pltpu.VMEM)
    return pl.pallas_call(
        relay_kernel,
        name="relay",
        out_shape=(
            jax.ShapeDtypeStruct((spans, SPAN, inner), BF16),
            jax.ShapeDtypeStruct((RING,) + item, BF16),
            jax.ShapeDtypeStruct((24, 128), jnp.int32),
            jax.ShapeDtypeStruct((1, 1), jnp.int32),
        ),
        in_specs=[any_spec] * 4 + [vmem_spec] * 2,
        out_specs=(any_spec, any_spec, vmem_spec, pl.BlockSpec(memory_space=pltpu.SMEM)),
        scratch_shapes=[
            pltpu.VMEM((spans, SPAN, inner), BF16),
            pltpu.VMEM((spans, NB * NBLEN, kvw2), BF16),
            pltpu.VMEM((2, spans, SPAN, inner), BF16),
            pltpu.VMEM((spans, SPAN, inner), BF16),
            pltpu.VMEM((2, HALF, kvw2), BF16),
            pltpu.VMEM((3, NB * NBLEN, kvw2), BF16),
            pltpu.VMEM(item, BF16),
            pltpu.VMEM(item, BF16),
            pltpu.VMEM(item, BF16),
            pltpu.VMEM((RING**3, NB, 128), jnp.int32),
            dma((spans, 2)),
            dma(()),
            dma((spans,)),
            dma((spans,)),
            dma((2, spans)),
            dma((spans,)),
            dma((spans,)),
            dma((spans,)),
            dma((spans, 3, 2)),
            dma((spans, 3, 2)),
            dma((spans, 3, 2)),
            dma((spans, 3, 2)),
            dma((3, 3)),
            dma((3, 3)),
        ],
        compiler_params=pltpu.CompilerParams(
            collective_id=0, has_side_effects=True, vmem_limit_bytes=60 * 2**20
        ),
        cost_estimate=pl.CostEstimate(flops=7 * 10**9, bytes_accessed=20 * 10**6, transcendentals=2**21),
    )(
        queries.reshape(spans, SPAN, inner),
        nb_kv.reshape(spans, NB * NBLEN, kvw2),
        out_grad.reshape(spans, SPAN, inner),
        weight.reshape(2, HALF, kvw2),
        owners.T,
        rows.T,
    )


def route_kernel(cap, table, gath_hbm, out_ref, prefix, *refs):
    names = ("gath", "msend", "mrecv", "psend", "rtrans", "rrecv")
    count_of = len(PIECES)
    buf = {name: refs[count_of * i : count_of * (i + 1)] for i, name in enumerate(names)}
    sems = refs[count_of * len(names) :]
    ld_sem, sems = sems[0], [sems[1 + 2 * i : 3 + 2 * i] for i in range(6)]
    stay, slots, passed = cap
    total = RING * stay
    near = neighbours()
    base = 0 if cap == FAST else 12
    first, second = range(3), range(3, 6)

    def load(q):
        _, begin, size = PIECES[q]
        return pltpu.make_async_copy(gath_hbm.at[:, pl.ds(begin, size)], buf["gath"][q], ld_sem.at[q])

    def remote(q, way, axis, src, dst, kind):
        send, recv = sems[kind]
        return pltpu.make_async_remote_copy(
            src, dst, send.at[q, way], recv.at[q, way],
            device_id=near[(PIECES[q][0] + axis) % 3][way], device_id_type=MESH,
        )

    def mid_first(q, way):
        return remote(q, way, 1, buf["msend"][q].at[pl.ds(way * slots, passed)],
                      buf["mrecv"][q].at[pl.ds(stay + way * slots, passed)], 0)

    def mid_rest(q, way):
        rest = slots - passed
        return remote(q, way, 1, buf["msend"][q].at[pl.ds(way * slots + passed, rest)],
                      buf["mrecv"][q].at[pl.ds(stay + way * slots + passed, rest)], 1)

    def mid_pass(q, way):
        return remote(q, way, 1, buf["mrecv"][q].at[pl.ds(stay + way * slots, passed)],
                      buf["mrecv"][q].at[pl.ds(stay + 2 * slots + way * passed, passed)], 2)

    def far(q, way):
        return remote(q, way, 2, buf["psend"][q].at[pl.ds(32 + 8 * way, 8)], buf["rtrans"][q].at[way], 3)

    def near_now(q, way):
        d = 1 + 2 * way
        part = 8 * (1 - way)
        return remote(q, way, 2, buf["psend"][q].at[pl.ds(16 * d + part, 8)],
                      buf["rrecv"][q].at[way, pl.ds(part, 8)], 4)

    def near_late(q, way):
        d = 1 + 2 * way
        part = 8 * way
        return remote(q, way, 2, buf["psend"][q].at[pl.ds(16 * d + part, 8)],
                      buf["rrecv"][q].at[way, pl.ds(part, 8)], 5)

    for q in range(count_of):
        load(q).start()
    greet([d for pair in near for d in pair])
    prefix[total] = jnp.zeros(prefix.shape[1:], BF16)

    def fill(q, name, begin, number, entry):
        def body(j, carry):
            index = table[base + PIECES[q][0] * 4, entry + j]
            buf[name][q][begin + j] = buf["gath"][q][index]
            return carry

        lax.fori_loop(0, number, body, 0)

    def send_first(q):
        for way in range(2):
            fill(q, "msend", way * slots, passed, stay + way * slots)
            mid_first(q, way).start()

    def send_rest(q):
        if slots > passed:
            for way in range(2):
                fill(q, "msend", way * slots + passed, slots - passed, stay + way * slots + passed)
                mid_rest(q, way).start()

    def pass_on(q):
        for way in range(2):
            mid_first(q, way).wait_recv()
            mid_pass(q, way).start()

    def reduce(q):
        part, _, size = PIECES[q]
        for way in range(2):
            if slots > passed:
                mid_rest(q, way).wait_recv()
            mid_pass(q, way).wait_recv()

        def run(n, acc):
            value = buf["mrecv"][q][table[base + part * 4 + 1, n]].astype(F32)
            acc = acc * table[base + part * 4 + 2, n].astype(F32) + value
            prefix[n, pl.ds(0, size)] = acc.astype(BF16)
            return acc

        lax.fori_loop(0, total, run, jnp.zeros((size, 128), F32))

        def rows(d):
            def body(r, carry):
                index = table[base + part * 4 + 3, d * 16 + r]
                buf["psend"][q][d * 16 + r] = prefix[index, pl.ds(0, size)]
                return carry

            lax.fori_loop(0, ROWS_DEV, body, 0)

        rows(2)
        far(q, 0).start()
        far(q, 1).start()
        rows(1)
        near_now(q, 0).start()
        rows(3)
        near_now(q, 1).start()
        rows(0)

    def join(q):
        for way in range(2):
            far(q, way).wait_recv()
            start = 16 * (1 + 2 * way) + 8 * way

            def add(r, carry):
                buf["psend"][q][start + r] = (
                    buf["psend"][q][start + r].astype(F32) + buf["rtrans"][q][way, r].astype(F32)
                ).astype(BF16)
                return carry

            lax.fori_loop(0, 8, add, 0)
            near_late(q, way).start()

    def finish(q):
        _, begin, size = PIECES[q]
        for way in range(2):
            near_now(q, way).wait_recv()
            near_late(q, way).wait_recv()

        def final(r, carry):
            out_ref[r, pl.ds(begin, size)] = (
                buf["psend"][q][r].astype(F32)
                + buf["rrecv"][q][0, r].astype(F32)
                + buf["rrecv"][q][1, r].astype(F32)
            ).astype(BF16)
            return carry

        lax.fori_loop(0, ROWS_DEV, final, 0)

    for q in first:
        load(q).wait()
        send_first(q)
    for q in first:
        send_rest(q)
    for q in second:
        load(q).wait()
        send_first(q)
    for q in first:
        pass_on(q)
    for q in second:
        send_rest(q)
    for q in range(count_of):
        fill(q, "mrecv", 0, stay, 0)
    for q in second:
        pass_on(q)
    for q in range(count_of):
        reduce(q)
    for q in range(count_of):
        join(q)
    for q in range(count_of):
        finish(q)
    for q in range(count_of):
        for way in range(2):
            mid_first(q, way).wait_send()
            if slots > passed:
                mid_rest(q, way).wait_send()
            mid_pass(q, way).wait_send()
            far(q, way).wait_send()
            near_now(q, way).wait_send()
            near_late(q, way).wait_send()


def route(cap, ident, gathered, table):
    items = gathered.shape[0]
    stay, slots, passed = cap
    sizes = [size for _, _, size in PIECES]
    dma = pltpu.SemaphoreType.DMA

    def per_piece(*lead):
        return [pltpu.VMEM(lead + (size, 128), BF16) for size in sizes]

    return pl.pallas_call(
        functools.partial(route_kernel, cap),
        name="route%d" % slots,
        out_shape=jax.ShapeDtypeStruct((ROWS_DEV, HALF, 128), BF16),
        in_specs=[pl.BlockSpec(memory_space=pltpu.SMEM), pl.BlockSpec(memory_space=pl.ANY)],
        out_specs=pl.BlockSpec(memory_space=pltpu.VMEM),
        scratch_shapes=[pltpu.VMEM((RING * stay + 1, max(sizes), 128), BF16)]
        + per_piece(items)
        + per_piece(2 * slots)
        + per_piece(stay + 2 * slots + 2 * passed)
        + per_piece(64)
        + per_piece(2, 8)
        + per_piece(2, ROWS_DEV)
        + [dma((len(sizes),))]
        + [dma((len(sizes), 2))] * 12,
        compiler_params=pltpu.CompilerParams(
            collective_id=ident, has_side_effects=True, vmem_limit_bytes=60 * 2**20
        ),
        cost_estimate=pl.CostEstimate(flops=10**7, bytes_accessed=10**7, transcendentals=0),
    )(table, gathered)


def hand_out_kernel(grad, enc, grad_out, enc_out, grad_v, in_sem, out_sem, enc_sem):
    count_of = grad.shape[0]
    ins = [pltpu.make_async_copy(grad.at[i], grad_v.at[i], in_sem.at[i]) for i in range(count_of)]
    outs = [pltpu.make_async_copy(grad_v.at[i], grad_out.at[i], out_sem.at[i]) for i in range(count_of)]
    encs = []
    for i in range(4):
        some = pl.ds(i * (ROWS_DEV // 4), ROWS_DEV // 4)
        encs.append(pltpu.make_async_copy(enc.at[some], enc_out.at[some], enc_sem.at[i]))
    for copy in ins + encs:
        copy.start()
    for copy, out in zip(ins, outs):
        copy.wait()
        out.start()
    for copy in encs + outs:
        copy.wait()


def hand_out(grad, enc):
    any_spec = pl.BlockSpec(memory_space=pl.ANY)
    dma = pltpu.SemaphoreType.DMA
    return pl.pallas_call(
        hand_out_kernel,
        name="hand_out",
        out_shape=(jax.ShapeDtypeStruct(grad.shape, grad.dtype), jax.ShapeDtypeStruct(enc.shape, enc.dtype)),
        in_specs=[any_spec, pl.BlockSpec(memory_space=pltpu.VMEM)],
        out_specs=(any_spec,) * 2,
        scratch_shapes=[
            pltpu.VMEM(grad.shape, grad.dtype), dma((grad.shape[0],)), dma((grad.shape[0],)), dma((4,))
        ],
        compiler_params=pltpu.CompilerParams(vmem_limit_bytes=60 * 2**20),
        cost_estimate=pl.CostEstimate(flops=0, bytes_accessed=8 * 10**6, transcendentals=0),
    )(grad, enc)


def local(queries, nb_kv, out_grad, kv_weight, nb_owner, nb_row):
    input_grad, gathered, table, most = relay(queries[0], nb_kv[0], out_grad, kv_weight[0], nb_owner, nb_row)
    gathered = gathered.reshape(-1, HALF, 128)
    packed = lax.cond(
        most[0, 0] == 0,
        lambda t, g: route(FAST, 1, g, t),
        lambda t, g: route(FULL, 2, g, t),
        table,
        gathered,
    )
    input_grad, packed = hand_out(input_grad, packed)
    return (input_grad.reshape(queries.shape), packed.swapaxes(1, 2))


def solution(mesh):
    in_specs = (
        P("section", "ctx", None),
        P("section", "ctx", None, None, None),
        P("ctx", None),
        P("section", None, None),
        P("ctx", None),
        P("ctx", None),
    )
    out_specs = (P("section", "ctx", None), P("ctx", None, "section"))
    return jax.shard_map(local, mesh=mesh, in_specs=in_specs, out_specs=out_specs, check_vma=False)
```
